512 devices in a mesh: group: 16 (over y, z_hi), expert: 32 (over x, z_lo, core).
Axes of the slice: x: 4, y: 4, z: 16 (z_hi: 4, z_lo: 4; z = z_hi * 4 + z_lo), core: 2. Of those that a mesh axis runs over, the one named last changes fastest.
Arguments:
- patches: bfloat16 [131072, 640], P(('group', 'expert')), may hold values from -8 to 8
- slot_params: bfloat16 [640, 256], replicated, may hold values from -5 to 5
- up_weight: bfloat16 [32, 640, 2560], P('expert', None, 'group'), may hold values from -0.25 to 0.25
- down_weight: bfloat16 [32, 2560, 640], P('expert', 'group'), may hold values from -0.125 to 0.125
- output_grad: bfloat16 [131072, 640], P(('group', 'expert')), may hold values from -6 to 6
Outputs:
- input_grad: bfloat16 [131072, 640], P(('group', 'expert'))
- slot_params_grad: float32 [640, 256], replicated
- up_grad: bfloat16 [32, 640, 2560], P('expert', 'group')
The draws below stay inside these ranges and needn't reach their ends.
All inputs are finite; a program needn't handle non-finite values.
Results may differ from the reference program's by a relative error of at most 0.018.
Values may be sent and summed in bfloat16 or wider, within the bound.
No kernel may reach another device: no remote copies, remote signals or barrier semaphores. Data moves between devices by JAX's collectives and lax.ppermute only.
A program may use at most 64 MiB of HBM per device.

```python
import math
import jax
import jax.numpy as jnp
from jax import lax

D = 640
FF = 2560
PATCHES = 256
SLOT_EXP = 8
IMG_DEV = 1
EXPERTS = 32
SLOTS = 256
IMAGES = 512
TOKENS = 131072
N_GROUP = 16
N_EXPERT = 32


def shared_fields(key):
    keys = jax.random.split(key, 8)
    normal_rows = jax.random.normal(keys[0], (TOKENS, D), jnp.float32)
    base_rows = normal_rows
    row_scale = jnp.exp(jax.random.uniform(keys[2], (TOKENS, 1), jnp.float32, math.log(0.3), math.log(3.0)))
    rows_field = base_rows * row_scale
    normal_cols = jax.random.normal(keys[3], (D, SLOTS), jnp.float32)
    base_cols = normal_cols
    col_scale = jnp.exp(jax.random.uniform(keys[5], (1, SLOTS), jnp.float32, math.log(0.3), math.log(3.0)))
    cols_field = base_cols * col_scale / math.sqrt(D)
    quarter = IMAGES // 4
    picked = jnp.arange(4, dtype=jnp.int32) * quarter + jax.random.randint(keys[6], (4,), 0, quarter)
    token_keys = jax.random.split(keys[7], 3)
    first_token = jax.random.randint(token_keys[0], (4,), 0, PATCHES)
    second_token = (first_token + 1 + jax.random.randint(token_keys[1], (4,), 0, PATCHES - 1)) % PATCHES
    slot_pick = jax.random.permutation(token_keys[2], SLOTS)[:8]
    rows_first = picked * PATCHES + first_token
    rows_second = picked * PATCHES + second_token
    now_first = rows_field[rows_first]
    rows_field = rows_field.at[rows_first].set(now_first)
    now_second = rows_field[rows_second]
    rows_field = rows_field.at[rows_second].set(now_second)
    slots_first = slot_pick[:4]
    slots_second = slot_pick[4:]
    now_cols = cols_field[:, slots_first]
    cols_field = cols_field.at[:, slots_first].set(now_cols)
    now_cols = cols_field[:, slots_second]
    cols_field = cols_field.at[:, slots_second].set(now_cols)
    return (jnp.clip(rows_field, -8.0, 8.0), jnp.clip(cols_field, -5.0, 5.0))


def draw_patches(key, part):
    rows_field, cols_field = shared_fields(key)
    return rows_field.astype(jnp.bfloat16)


def draw_slot_params(key, part):
    rows_field, cols_field = shared_fields(key)
    return cols_field.astype(jnp.bfloat16)


def shard_levels(rng, dims, pieces, low, high):
    factor_of, own = 1.0, jax.random.fold_in(rng, 6)
    for dim, shards_of in pieces:
        steps = jnp.exp(jax.random.uniform(jax.random.fold_in(own, dim), (shards_of,), jnp.float32, low / len(pieces), high / len(pieces)))
        factor_of = factor_of * jnp.repeat(steps, dims[dim] // shards_of).reshape([-1 if axis == dim else 1 for axis in range(len(dims))])
    return factor_of


def scatter_about(own_key, shape, deviation, limit, cuts=(), kind=jnp.bfloat16):
    values = deviation * jax.random.normal(own_key, shape, jnp.float32)
    if cuts:
        values = values * shard_levels(own_key, shape, cuts, -0.22, 0.18)
    return jnp.clip(values, -limit, limit).astype(kind)


def setup_inputs(seed: int = 0) -> dict:
    streams_of = jax.random.split(jax.random.key(seed), 6)
    patches = draw_patches(jax.random.fold_in(streams_of[5], 71), 0)
    slot_params = draw_slot_params(jax.random.fold_in(streams_of[5], 71), 0)
    up_weight = scatter_about(streams_of[2], (EXPERTS, D, FF), D ** -0.5, 0.25, ((0, 32), (2, 16)))
    down_weight = scatter_about(streams_of[3], (EXPERTS, FF, D), FF ** -0.5, 0.125, ((0, 32), (1, 16)))
    output_grad = scatter_about(streams_of[4], (TOKENS, D), 1.0, 6.0, ((0, 512),))
    return {"patches": patches, "slot_params": slot_params, "up_weight": up_weight, "down_weight": down_weight, "output_grad": output_grad}


cubic_coef = 0.044715
sqrt_ratio = 0.7978845608028654

def gelu_value(values):
    inner = sqrt_ratio * (values + cubic_coef * values * values * values)
    return 0.5 * values * (1.0 + jnp.tanh(inner))

def gelu_slope(values):
    tangent = jnp.tanh(sqrt_ratio * (values + cubic_coef * values * values * values))
    return 0.5 * (1.0 + tangent) + 0.5 * values * (1.0 - tangent * tangent) * sqrt_ratio * (1.0 + 3.0 * cubic_coef * values * values)

def weights_of(image_rows, slot_params):
    logits = jnp.dot(image_rows, slot_params, preferred_element_type=jnp.float32)
    dispatch = jax.nn.softmax(logits, axis=0)
    combine = jax.nn.softmax(logits, axis=1)
    return (dispatch, combine)

def image_front(items, slot_params):
    image_rows, grad_rows = items
    dispatch, combine = weights_of(image_rows, slot_params)
    dispatch_low = dispatch.astype(jnp.bfloat16)
    combine_low = combine.astype(jnp.bfloat16)
    slots_in = jnp.dot(dispatch_low.T, image_rows, preferred_element_type=jnp.float32).astype(jnp.bfloat16)
    slot_grads = jnp.dot(combine_low.T, grad_rows, preferred_element_type=jnp.float32).astype(jnp.bfloat16)
    return (slots_in, slot_grads)

def expert_work(items):
    up_mat, down_mat, rows_in, grads_in = items
    up_wide = up_mat.astype(jnp.float32)
    down_wide = down_mat.astype(jnp.float32)
    rows_wide = rows_in.astype(jnp.float32)
    hidden = jnp.einsum('grd,df->grf', rows_wide, up_wide)
    activation = gelu_value(hidden).astype(jnp.bfloat16)
    expert_out = jnp.einsum('grf,fd->grd', activation.astype(jnp.float32), down_wide).astype(jnp.bfloat16)
    act_grad = jnp.einsum('grd,fd->grf', grads_in.astype(jnp.float32), down_wide)
    hidden_grad = (act_grad * gelu_slope(hidden)).astype(jnp.bfloat16)
    hidden_wide = hidden_grad.astype(jnp.float32)
    rows_grad = jnp.einsum('grf,df->grd', hidden_wide, up_wide).astype(jnp.bfloat16)
    terms = jnp.einsum('grd,grf->gdf', rows_wide, hidden_wide).astype(jnp.bfloat16)
    terms = lax.optimization_barrier(terms)
    up_total = lax.optimization_barrier(jnp.sum(terms.astype(jnp.float32), axis=0)).astype(jnp.bfloat16)
    return (expert_out, rows_grad, up_total)

def by_expert(values):
    shaped = values.reshape(N_GROUP, N_EXPERT * IMG_DEV, EXPERTS, SLOT_EXP, D)
    return shaped.transpose(2, 0, 1, 3, 4).reshape(EXPERTS, N_GROUP, N_EXPERT * IMG_DEV * SLOT_EXP, D)

def by_image(values):
    shaped = values.reshape(EXPERTS, N_GROUP, N_EXPERT * IMG_DEV, SLOT_EXP, D)
    return shaped.transpose(1, 2, 0, 3, 4).reshape(IMAGES, SLOTS, D)

def reference(patches, slot_params, up_weight, down_weight, output_grad):
    images = patches.reshape(IMAGES, PATCHES, D)
    grads = output_grad.reshape(IMAGES, PATCHES, D)

    def front(items):
        return image_front(items, slot_params)
    slots_in, slot_grads = lax.map(front, (images, grads))
    expert_out, rows_grad, up_grad = lax.map(expert_work, (up_weight, down_weight, by_expert(slots_in), by_expert(slot_grads)))
    slot_out = by_image(expert_out)
    slot_in_grad = by_image(rows_grad)

    def image_back(total, items):
        image_rows, grad_rows, out_rows, in_grad = items
        dispatch, combine = weights_of(image_rows, slot_params)
        dispatch_low = dispatch.astype(jnp.bfloat16)
        dcombine = jnp.dot(grad_rows, out_rows.T, preferred_element_type=jnp.float32)
        ddispatch = jnp.dot(image_rows, in_grad.T, preferred_element_type=jnp.float32)
        logit_grad = dispatch * (ddispatch - lax.optimization_barrier(jnp.sum(dispatch * ddispatch, axis=0, keepdims=True)))
        logit_grad = logit_grad + combine * (dcombine - lax.optimization_barrier(jnp.sum(combine * dcombine, axis=1, keepdims=True)))
        logit_low = logit_grad.astype(jnp.bfloat16)
        image_grad = jnp.dot(dispatch_low, in_grad, preferred_element_type=jnp.float32)
        image_grad = image_grad + jnp.dot(logit_low, slot_params.T, preferred_element_type=jnp.float32)
        total = total + jnp.dot(image_rows.T, logit_low, preferred_element_type=jnp.float32)
        return (total, image_grad.astype(jnp.bfloat16))
    phi_grad, input_grad = lax.scan(image_back, jnp.zeros((D, SLOTS), jnp.float32), (images, grads, slot_out, slot_in_grad))
    return (input_grad.reshape(TOKENS, D), phi_grad, up_grad)
```

```python
import jax
import jax.numpy as jnp
from jax import lax
from jax.sharding import Mesh, PartitionSpec as P

SLOT_EXP = 8
SIZES = {"y": 4, "h": 4, "x": 4, "l": 4, "c": 2}
AXES = ("y", "h", "x", "l", "c")
OWNERS = ("x", "l", "c")

cubic_coef = 0.044715
sqrt_ratio = 0.7978845608028654


def gelu_value(values):
    inner = sqrt_ratio * (values + cubic_coef * values * values * values)
    return 0.5 * values * (1.0 + jnp.tanh(inner))


def gelu_slope(values):
    tangent = jnp.tanh(sqrt_ratio * (values + cubic_coef * values * values * values))
    return 0.5 * (1.0 + tangent) + 0.5 * values * (1.0 - tangent * tangent) * sqrt_ratio * (
        1.0 + 3.0 * cubic_coef * values * values
    )


def mul(a, b, dims):
    return lax.dot_general(a, b, (dims, ((), ())), preferred_element_type=jnp.float32)


def shift(values, axis, step):
    size = lax.axis_size(axis)
    return lax.ppermute(values, axis, [(i, (i + step) % size) for i in range(size)])


def gather_hidden(weights):
    here = lax.axis_index("h")
    low = shift(weights, "h", 1)
    high = shift(weights, "h", -1)
    up_far = shift(low[0], "h", 1)
    down_far = shift(high[1], "h", -1)
    far = jnp.stack([up_far, down_far])
    full = jnp.zeros((2, 4) + weights.shape[1:], weights.dtype)
    for block, offset in ((weights, 0), (low, 3), (high, 1), (far, 2)):
        full = lax.dynamic_update_slice_in_dim(full, block[:, None], (here + offset) % 4, 1)
    return full


def everywhere(values, axes, count):
    spread = jnp.broadcast_to(values[None], (count,) + values.shape)
    return lax.all_to_all(spread, axes, 0, 0)


def local(patches, slot_params, up_weight, down_weight, output_grad):
    width = patches.shape[1]
    slots = slot_params.shape[1]
    owners = slots // SLOT_EXP
    shard = up_weight.shape[2]
    low = jnp.bfloat16

    weights = jnp.stack([up_weight[0].T, down_weight[0]])
    full = gather_hidden(weights).reshape(2, 4 * shard, width)
    up_rows, down_rows = full[0], full[1]

    logits = mul(patches, slot_params, ((1,), (0,)))
    dispatch = jax.nn.softmax(logits, axis=0)
    combine = jax.nn.softmax(logits, axis=1)
    dispatch_low = dispatch.astype(low)
    combine_low = combine.astype(low)
    slots_in = mul(dispatch_low, patches, ((0,), (0,))).astype(low)
    slot_grads = mul(combine_low, output_grad, ((0,), (0,))).astype(low)

    both = jnp.stack([slots_in, slot_grads]).reshape(2, owners, SLOT_EXP, width)
    landed = lax.all_to_all(both, OWNERS, 1, 1, tiled=True).reshape(2, slots, width)
    rows = everywhere(landed, "y", 4)
    rows_in = rows[:, 0].reshape(4 * slots, width)
    grads_in = rows[:, 1].reshape(4 * slots, width)

    hidden = mul(rows_in, up_rows, ((1,), (1,)))
    act_grad = mul(grads_in, down_rows, ((1,), (1,)))
    activation = gelu_value(hidden).astype(low)
    hidden_grad = (act_grad * gelu_slope(hidden)).astype(low)
    part_out = mul(activation, down_rows, ((1,), (0,))).astype(low)
    part_in = mul(hidden_grad, up_rows, ((1,), (0,))).astype(low)
    parts = jnp.stack([part_out.reshape(4, slots, width), part_in.reshape(4, slots, width)], axis=1)
    summed = jnp.sum(lax.all_to_all(parts, "y", 0, 0).astype(jnp.float32), axis=0).astype(low)
    back = lax.all_to_all(
        summed.reshape(2, owners, SLOT_EXP, width), OWNERS, 1, 1, tiled=True
    ).reshape(2, slots, width)
    slot_out, slot_in_grad = back[0], back[1]

    up_term = mul(rows_in, hidden_grad, ((0,), (0,))).astype(low)
    up_term = up_term.reshape(4, 4, width // 16, 4 * shard)
    up_term = lax.all_to_all(up_term, "h", 1, 0)
    up_sum = jnp.sum(up_term.astype(jnp.float32), axis=0).astype(low)
    up_grad = lax.all_to_all(up_sum, "y", 0, 0)
    up_grad = jnp.transpose(up_grad, (1, 0, 2)).reshape(1, width // 16, 16 * shard)

    dcombine = mul(output_grad, slot_out, ((1,), (1,)))
    ddispatch = mul(patches, slot_in_grad, ((1,), (1,)))
    logit_grad = dispatch * (ddispatch - jnp.sum(dispatch * ddispatch, axis=0, keepdims=True))
    logit_grad = logit_grad + combine * (
        dcombine - jnp.sum(combine * dcombine, axis=1, keepdims=True)
    )
    logit_low = logit_grad.astype(low)

    phi_term = mul(patches, logit_low, ((0,), (0,))).astype(low)
    pieces = SIZES["y"] * SIZES["x"] * SIZES["c"]
    piece = phi_term.reshape(pieces, width // pieces, slots)
    piece = jnp.sum(lax.all_to_all(piece, ("y", "x", "c"), 0, 0).astype(jnp.float32), axis=0)
    piece = everywhere(piece.astype(low), ("h", "l"), SIZES["h"] * SIZES["l"])
    piece = jnp.sum(piece.astype(jnp.float32), axis=0)
    phi_grad = everywhere(piece.astype(low), ("y", "x", "c"), pieces)
    phi_grad = phi_grad.reshape(width, slots).astype(jnp.float32)

    image_grad = mul(dispatch_low, slot_in_grad, ((1,), (0,)))
    image_grad = image_grad + mul(logit_low, slot_params, ((1,), (1,)))
    return image_grad.astype(low), phi_grad, up_grad


def solution(mesh):
    fine = Mesh(mesh.devices.reshape([SIZES[name] for name in AXES]), AXES)
    group = ("y", "h")
    placed = (
        P(AXES, None),
        P(),
        P(OWNERS, None, group),
        P(OWNERS, group, None),
        P(AXES, None),
    )
    return jax.shard_map(
        local,
        mesh=fine,
        in_specs=placed,
        out_specs=(P(AXES, None), P(), P(OWNERS, group, None)),
        check_vma=False,
    )
```

```python
import jax
import jax.numpy as jnp
from jax import lax
from jax.sharding import Mesh, PartitionSpec as P

SLOT_EXP = 8
SIZES = {"y": 4, "h": 4, "x": 4, "l": 4, "c": 2}
AXES = ("y", "h", "x", "l", "c")
OWNERS = ("x", "l", "c")

cubic_coef = 0.044715
sqrt_ratio = 0.7978845608028654


def gelu_value(values):
    inner = sqrt_ratio * (values + cubic_coef * values * values * values)
    return 0.5 * values * (1.0 + jnp.tanh(inner))


def gelu_slope(values):
    tangent = jnp.tanh(sqrt_ratio * (values + cubic_coef * values * values * values))
    return 0.5 * (1.0 + tangent) + 0.5 * values * (1.0 - tangent * tangent) * sqrt_ratio * (
        1.0 + 3.0 * cubic_coef * values * values
    )


def mul(a, b, dims):
    return lax.dot_general(a, b, (dims, ((), ())), preferred_element_type=jnp.float32)


def shift(values, axis, step):
    size = lax.axis_size(axis)
    return lax.ppermute(values, axis, [(i, (i + step) % size) for i in range(size)])


def gather_hidden(weights, low, high):
    here = lax.axis_index("h")
    up_far = shift(low[0], "h", 1)
    down_far = shift(high[1], "h", -1)
    far = jnp.stack([up_far, down_far])
    full = jnp.zeros((2, 4) + weights.shape[1:], weights.dtype)
    for block, offset in ((weights, 0), (low, 3), (high, 1), (far, 2)):
        full = lax.dynamic_update_slice_in_dim(full, block[:, None], (here + offset) % 4, 1)
    return full


def sum_hidden(terms):
    here = lax.axis_index("h")

    def chunk(offset):
        return lax.dynamic_index_in_dim(terms, (here + offset) % 4, 1, keepdims=False)

    def add(one, other):
        return (one.astype(jnp.float32) + other.astype(jnp.float32)).astype(terms.dtype)

    far, right, left = chunk(2), chunk(1), chunk(3)
    far_right = shift(far[:2], "h", 1)
    far_left = shift(far[2:], "h", -1)
    right = shift(jnp.concatenate([add(right[:2], far_right), right[2:]]), "h", 1)
    left = shift(jnp.concatenate([left[:2], add(left[2:], far_left)]), "h", -1)
    total = chunk(0).astype(jnp.float32) + right.astype(jnp.float32) + left.astype(jnp.float32)
    return total.astype(terms.dtype)


def everywhere(values, axes, count):
    spread = jnp.broadcast_to(values[None], (count,) + values.shape)
    return lax.all_to_all(spread, axes, 0, 0)


def local(patches, slot_params, up_weight, down_weight, output_grad):
    width = patches.shape[1]
    slots = slot_params.shape[1]
    owners = slots // SLOT_EXP
    shard = up_weight.shape[2]
    low = jnp.bfloat16

    weights = jnp.stack([up_weight[0].T, down_weight[0]])
    from_low = shift(weights, "h", 1)
    from_high = shift(weights, "h", -1)

    logits = mul(patches, slot_params, ((1,), (0,)))
    dispatch = jax.nn.softmax(logits, axis=0)
    combine = jax.nn.softmax(logits, axis=1)
    dispatch_low = dispatch.astype(low)
    combine_low = combine.astype(low)
    slots_in = mul(dispatch_low, patches, ((0,), (0,))).astype(low)
    slot_grads = mul(combine_low, output_grad, ((0,), (0,))).astype(low)

    both = jnp.stack([slots_in, slot_grads]).reshape(2, owners, SLOT_EXP, width)
    landed = lax.all_to_all(both, OWNERS, 1, 1, tiled=True).reshape(2, slots, width)
    landed, from_low, from_high = lax.optimization_barrier((landed, from_low, from_high))
    full = gather_hidden(weights, from_low, from_high).reshape(2, 4 * shard, width)
    up_rows, down_rows = full[0], full[1]
    rows = everywhere(landed, "y", 4)
    rows_in = rows[:, 0].reshape(4 * slots, width)
    grads_in = rows[:, 1].reshape(4 * slots, width)

    hidden = mul(rows_in, up_rows, ((1,), (1,)))
    act_grad = mul(grads_in, down_rows, ((1,), (1,)))
    activation = gelu_value(hidden).astype(low)
    hidden_grad = (act_grad * gelu_slope(hidden)).astype(low)
    part_out = mul(activation, down_rows, ((1,), (0,))).astype(low)
    part_in = mul(hidden_grad, up_rows, ((1,), (0,))).astype(low)
    parts = jnp.stack([part_out.reshape(4, slots, width), part_in.reshape(4, slots, width)], axis=1)
    summed = jnp.sum(lax.all_to_all(parts, "y", 0, 0).astype(jnp.float32), axis=0).astype(low)
    back = lax.all_to_all(
        summed.reshape(2, owners, SLOT_EXP, width), OWNERS, 1, 1, tiled=True
    ).reshape(2, slots, width)
    slot_out, slot_in_grad = back[0], back[1]

    up_term = mul(rows_in, hidden_grad, ((0,), (0,))).astype(low)
    up_term = up_term.reshape(4, 4, width // 16, 4 * shard)
    up_sum = sum_hidden(up_term)
    up_grad = lax.all_to_all(up_sum, "y", 0, 0)
    up_grad = jnp.transpose(up_grad, (1, 0, 2)).reshape(1, width // 16, 16 * shard)

    dcombine = mul(output_grad, slot_out, ((1,), (1,)))
    ddispatch = mul(patches, slot_in_grad, ((1,), (1,)))
    logit_grad = dispatch * (ddispatch - jnp.sum(dispatch * ddispatch, axis=0, keepdims=True))
    logit_grad = logit_grad + combine * (
        dcombine - jnp.sum(combine * dcombine, axis=1, keepdims=True)
    )
    logit_low = logit_grad.astype(low)

    phi_term = mul(patches, logit_low, ((0,), (0,))).astype(low)
    pieces = SIZES["y"] * SIZES["x"] * SIZES["c"]
    piece = phi_term.reshape(pieces, width // pieces, slots)
    piece = jnp.sum(lax.all_to_all(piece, ("y", "x", "c"), 0, 0).astype(jnp.float32), axis=0)
    piece = everywhere(piece.astype(low), ("h", "l"), SIZES["h"] * SIZES["l"])
    piece = jnp.sum(piece.astype(jnp.float32), axis=0)
    phi_grad = everywhere(piece.astype(low), ("y", "x", "c"), pieces)
    phi_grad = phi_grad.reshape(width, slots).astype(jnp.float32)

    image_grad = mul(dispatch_low, slot_in_grad, ((1,), (0,)))
    image_grad = image_grad + mul(logit_low, slot_params, ((1,), (1,)))
    return image_grad.astype(low), phi_grad, up_grad


def solution(mesh):
    fine = Mesh(mesh.devices.reshape([SIZES[name] for name in AXES]), AXES)
    group = ("y", "h")
    placed = (
        P(AXES, None),
        P(),
        P(OWNERS, None, group),
        P(OWNERS, group, None),
        P(AXES, None),
    )
    return jax.shard_map(
        local,
        mesh=fine,
        in_specs=placed,
        out_specs=(P(AXES, None), P(), P(OWNERS, group, None)),
        check_vma=False,
    )
```

```python
import jax
import jax.numpy as jnp
from jax import lax
from jax.sharding import Mesh, PartitionSpec as P

SLOT_EXP = 8
SIZES = {"y": 4, "h": 4, "x": 4, "l": 4, "c": 2}
AXES = ("y", "h", "x", "l", "c")
OWNERS = ("x", "l", "c")

cubic_coef = 0.044715
sqrt_ratio = 0.7978845608028654


def gelu_value(values):
    inner = sqrt_ratio * (values + cubic_coef * values * values * values)
    return 0.5 * values * (1.0 + jnp.tanh(inner))


def gelu_slope(values):
    tangent = jnp.tanh(sqrt_ratio * (values + cubic_coef * values * values * values))
    return 0.5 * (1.0 + tangent) + 0.5 * values * (1.0 - tangent * tangent) * sqrt_ratio * (
        1.0 + 3.0 * cubic_coef * values * values
    )


def mul(a, b, dims):
    return lax.dot_general(a, b, (dims, ((), ())), preferred_element_type=jnp.float32)


def shift(values, axis, step):
    size = lax.axis_size(axis)
    return lax.ppermute(values, axis, [(i, (i + step) % size) for i in range(size)])


ROW_PAIRS = (1, 0, 3, 2)
WEIGHT_PAIRS = (3, 2, 1, 0)


def swap(values, pairs):
    return lax.ppermute(values, "y", list(enumerate(pairs)))


def place(buffer, half, offset, block):
    index = (half, (lax.axis_index("h") + offset) % 4, 0, 0)
    return lax.dynamic_update_slice(buffer, block[None, None], index)


def sum_hidden(terms):
    here = lax.axis_index("h")

    def chunk(offset):
        return lax.dynamic_index_in_dim(terms, (here + offset) % 4, 1, keepdims=False)

    def add(one, other):
        return (one.astype(jnp.float32) + other.astype(jnp.float32)).astype(terms.dtype)

    far, right, left = chunk(2), chunk(1), chunk(3)
    far_right = shift(far[:2], "h", 1)
    far_left = shift(far[2:], "h", -1)
    right = shift(jnp.concatenate([add(right[:2], far_right), right[2:]]), "h", 1)
    left = shift(jnp.concatenate([left[:2], add(left[2:], far_left)]), "h", -1)
    total = chunk(0).astype(jnp.float32) + right.astype(jnp.float32) + left.astype(jnp.float32)
    return total.astype(terms.dtype)


def everywhere(values, axes, count):
    spread = jnp.broadcast_to(values[None], (count,) + values.shape)
    return lax.all_to_all(spread, axes, 0, 0)


def local(patches, slot_params, up_weight, down_weight, output_grad):
    width = patches.shape[1]
    slots = slot_params.shape[1]
    owners = slots // SLOT_EXP
    shard = up_weight.shape[2]
    low = jnp.bfloat16

    weights = jnp.stack([up_weight[0].T, down_weight[0]])
    from_low = shift(weights, "h", 1)
    from_high = shift(weights, "h", -1)
    partner = swap(weights, WEIGHT_PAIRS)

    logits = mul(patches, slot_params, ((1,), (0,)))
    dispatch = jax.nn.softmax(logits, axis=0)
    combine = jax.nn.softmax(logits, axis=1)
    dispatch_low = dispatch.astype(low)
    combine_low = combine.astype(low)
    slots_in = mul(dispatch_low, patches, ((0,), (0,))).astype(low)
    slot_grads = mul(combine_low, output_grad, ((0,), (0,))).astype(low)

    both = jnp.stack([slots_in, slot_grads]).reshape(2, owners, SLOT_EXP, width)
    both, from_low, from_high, partner = lax.optimization_barrier(
        (both, from_low, from_high, partner)
    )
    landed = lax.all_to_all(both, OWNERS, 1, 1, tiled=True).reshape(2, slots, width)
    up_far = shift(from_low[0], "h", 1)
    down_far = shift(from_high[1], "h", -1)
    partner_low = swap(from_low, WEIGHT_PAIRS)
    partner_high = swap(from_high, WEIGHT_PAIRS)
    landed, up_far, down_far, partner_low, partner_high = lax.optimization_barrier(
        (landed, up_far, down_far, partner_low, partner_high)
    )
    their_rows = swap(landed, ROW_PAIRS)
    far = (up_far, down_far)
    partner_far = (swap(up_far, WEIGHT_PAIRS), swap(down_far, WEIGHT_PAIRS))

    def assemble(which):
        buffer = jnp.zeros((2, 4, shard, width), low)
        for half, blocks in enumerate(
            (
                (weights[which], from_high[which], far[which], from_low[which]),
                (partner[which], partner_high[which], partner_far[which], partner_low[which]),
            )
        ):
            for offset, block in enumerate(blocks):
                buffer = place(buffer, half, offset, block)
        return buffer.reshape(8 * shard, width)

    up_rows, down_rows = assemble(0), assemble(1)

    def expert(rows_in, grads_in):
        hidden = mul(rows_in, up_rows, ((1,), (1,)))
        act_grad = mul(grads_in, down_rows, ((1,), (1,)))
        activation = gelu_value(hidden).astype(low)
        hidden_grad = (act_grad * gelu_slope(hidden)).astype(low)
        part_out = mul(activation, down_rows, ((1,), (0,)))
        part_in = mul(hidden_grad, up_rows, ((1,), (0,)))
        return hidden_grad, part_out, part_in

    their_hidden, their_out, their_in = expert(their_rows[0], their_rows[1])
    out_back = swap(their_out.astype(low), ROW_PAIRS)
    in_back = swap(their_in.astype(low), ROW_PAIRS)
    own_hidden, own_out, own_in = expert(landed[0], landed[1])
    summed = jnp.stack(
        [
            (own_out + out_back.astype(jnp.float32)).astype(low),
            (own_in + in_back.astype(jnp.float32)).astype(low),
        ]
    )
    back = lax.all_to_all(
        summed.reshape(2, owners, SLOT_EXP, width), OWNERS, 1, 1, tiled=True
    ).reshape(2, slots, width)
    slot_out, slot_in_grad = back[0], back[1]

    def up_half(half):
        columns = slice(half * 4 * shard, (half + 1) * 4 * shard)
        term = mul(landed[0], own_hidden[:, columns], ((0,), (0,)))
        return term + mul(their_rows[0], their_hidden[:, columns], ((0,), (0,)))

    up_other = swap(up_half(1).astype(low), WEIGHT_PAIRS)
    up_term = (up_half(0) + up_other.astype(jnp.float32)).astype(low)
    up_term = up_term.reshape(4, 4, width // 16, 4 * shard)
    up_sum = sum_hidden(up_term)
    up_grad = lax.all_to_all(up_sum, "y", 0, 0)
    up_grad = jnp.transpose(up_grad, (1, 0, 2)).reshape(1, width // 16, 16 * shard)

    dcombine = mul(output_grad, slot_out, ((1,), (1,)))
    ddispatch = mul(patches, slot_in_grad, ((1,), (1,)))
    logit_grad = dispatch * (ddispatch - jnp.sum(dispatch * ddispatch, axis=0, keepdims=True))
    logit_grad = logit_grad + combine * (
        dcombine - jnp.sum(combine * dcombine, axis=1, keepdims=True)
    )
    logit_low = logit_grad.astype(low)

    phi_term = mul(patches, logit_low, ((0,), (0,))).astype(low)
    pieces = SIZES["y"] * SIZES["x"] * SIZES["c"]
    piece = phi_term.reshape(pieces, width // pieces, slots)
    piece = jnp.sum(lax.all_to_all(piece, ("y", "x", "c"), 0, 0).astype(jnp.float32), axis=0)
    piece = everywhere(piece.astype(low), ("h", "l"), SIZES["h"] * SIZES["l"])
    piece = jnp.sum(piece.astype(jnp.float32), axis=0)
    phi_grad = everywhere(piece.astype(low), ("y", "x", "c"), pieces)
    phi_grad = phi_grad.reshape(width, slots).astype(jnp.float32)

    image_grad = mul(dispatch_low, slot_in_grad, ((1,), (0,)))
    image_grad = image_grad + mul(logit_low, slot_params, ((1,), (1,)))
    return image_grad.astype(low), phi_grad, up_grad


def solution(mesh):
    fine = Mesh(mesh.devices.reshape([SIZES[name] for name in AXES]), AXES)
    group = ("y", "h")
    placed = (
        P(AXES, None),
        P(),
        P(OWNERS, None, group),
        P(OWNERS, group, None),
        P(AXES, None),
    )
    return jax.shard_map(
        local,
        mesh=fine,
        in_specs=placed,
        out_specs=(P(AXES, None), P(), P(OWNERS, group, None)),
        check_vma=False,
    )
```

```python
import jax
import jax.numpy as jnp
from jax import lax
from jax.sharding import Mesh, PartitionSpec as P

SLOT_EXP = 8
SIZES = {"y": 4, "h": 4, "x": 4, "l": 4, "c": 2}
AXES = ("y", "h", "x", "l", "c")
OWNERS = ("x", "l", "c")

cubic_coef = 0.044715
sqrt_ratio = 0.7978845608028654


def gelu_value(values):
    inner = sqrt_ratio * (values + cubic_coef * values * values * values)
    return 0.5 * values * (1.0 + jnp.tanh(inner))


def gelu_slope(values):
    tangent = jnp.tanh(sqrt_ratio * (values + cubic_coef * values * values * values))
    return 0.5 * (1.0 + tangent) + 0.5 * values * (1.0 - tangent * tangent) * sqrt_ratio * (
        1.0 + 3.0 * cubic_coef * values * values
    )


def mul(a, b, dims):
    return lax.dot_general(a, b, (dims, ((), ())), preferred_element_type=jnp.float32)


def shift(values, axis, step):
    size = lax.axis_size(axis)
    return lax.ppermute(values, axis, [(i, (i + step) % size) for i in range(size)])


def sum_hidden(terms):
    here = lax.axis_index("h")

    def chunk(offset):
        return lax.dynamic_index_in_dim(terms, (here + offset) % 4, 1, keepdims=False)

    def add(one, other):
        return (one.astype(jnp.float32) + other.astype(jnp.float32)).astype(terms.dtype)

    far, right, left = chunk(2), chunk(1), chunk(3)
    far_right = shift(far[:2], "h", 1)
    far_left = shift(far[2:], "h", -1)
    right = shift(jnp.concatenate([add(right[:2], far_right), right[2:]]), "h", 1)
    left = shift(jnp.concatenate([left[:2], add(left[2:], far_left)]), "h", -1)
    total = chunk(0).astype(jnp.float32) + right.astype(jnp.float32) + left.astype(jnp.float32)
    return total.astype(terms.dtype)


def spread_rows(terms):
    here = lax.axis_index("y")
    result = jnp.zeros(terms.shape, terms.dtype)
    for step in range(4):
        block = lax.dynamic_index_in_dim(terms, (here + step) % 4, 0, keepdims=True)
        if step:
            block = shift(block, "y", step)
        result = lax.dynamic_update_slice_in_dim(result, block, (here - step) % 4, 0)
    return jnp.transpose(result, (1, 0, 2))


def everywhere(values, axes, count):
    spread = jnp.broadcast_to(values[None], (count,) + values.shape)
    return lax.all_to_all(spread, axes, 0, 0)


def local(patches, slot_params, up_weight, down_weight, output_grad):
    width = patches.shape[1]
    slots = slot_params.shape[1]
    owners = slots // SLOT_EXP
    shard = up_weight.shape[2]
    low = jnp.bfloat16

    logits = mul(patches, slot_params, ((1,), (0,)))
    dispatch = jax.nn.softmax(logits, axis=0)
    combine = jax.nn.softmax(logits, axis=1)
    dispatch_low = dispatch.astype(low)
    combine_low = combine.astype(low)
    slots_in = mul(dispatch_low, patches, ((0,), (0,))).astype(low)
    slot_grads = mul(combine_low, output_grad, ((0,), (0,))).astype(low)

    both = jnp.stack([slots_in, slot_grads]).reshape(2, owners, SLOT_EXP, width)
    landed = lax.all_to_all(both, OWNERS, 1, 1, tiled=True).reshape(2, slots, width)
    up_rows = lax.all_gather(up_weight[0].T, "h").reshape(4 * shard, width)
    landed, up_rows, down_rows = lax.optimization_barrier((landed, up_rows, down_weight[0]))
    down_rows = lax.all_gather(down_rows, "h").reshape(4 * shard, width)
    rows = everywhere(landed, "y", 4)
    rows_in = rows[:, 0].reshape(4 * slots, width)
    grads_in = rows[:, 1].reshape(4 * slots, width)

    hidden = mul(rows_in, up_rows, ((1,), (1,)))
    act_grad = mul(grads_in, down_rows, ((1,), (1,)))
    activation = gelu_value(hidden).astype(low)
    hidden_grad = (act_grad * gelu_slope(hidden)).astype(low)
    part_out = mul(activation, down_rows, ((1,), (0,))).astype(low)
    part_in = mul(hidden_grad, up_rows, ((1,), (0,))).astype(low)
    parts = jnp.stack([part_out.reshape(4, slots, width), part_in.reshape(4, slots, width)], axis=1)
    summed = jnp.sum(lax.all_to_all(parts, "y", 0, 0).astype(jnp.float32), axis=0).astype(low)
    up_term = mul(rows_in, hidden_grad, ((0,), (0,))).astype(low)
    up_sum = sum_hidden(up_term.reshape(4, 4, width // 16, 4 * shard))
    summed, up_sum = lax.optimization_barrier((summed, up_sum))
    up_grad = spread_rows(up_sum)
    back = lax.all_to_all(
        summed.reshape(2, owners, SLOT_EXP, width), OWNERS, 1, 1, tiled=True
    ).reshape(2, slots, width)
    slot_out, slot_in_grad = back[0], back[1]

    up_grad = up_grad.reshape(1, width // 16, 16 * shard)

    dcombine = mul(output_grad, slot_out, ((1,), (1,)))
    ddispatch = mul(patches, slot_in_grad, ((1,), (1,)))
    logit_grad = dispatch * (ddispatch - jnp.sum(dispatch * ddispatch, axis=0, keepdims=True))
    logit_grad = logit_grad + combine * (
        dcombine - jnp.sum(combine * dcombine, axis=1, keepdims=True)
    )
    logit_low = logit_grad.astype(low)

    phi_term = mul(patches, logit_low, ((0,), (0,))).astype(low)
    pieces = SIZES["y"] * SIZES["x"] * SIZES["c"]
    piece = phi_term.reshape(pieces, width // pieces, slots)
    piece = jnp.sum(lax.all_to_all(piece, ("y", "x", "c"), 0, 0).astype(jnp.float32), axis=0)
    piece = everywhere(piece.astype(low), ("h", "l"), SIZES["h"] * SIZES["l"])
    piece = jnp.sum(piece.astype(jnp.float32), axis=0)
    phi_grad = everywhere(piece.astype(low), ("y", "x", "c"), pieces)
    phi_grad = phi_grad.reshape(width, slots).astype(jnp.float32)

    image_grad = mul(dispatch_low, slot_in_grad, ((1,), (0,)))
    image_grad = image_grad + mul(logit_low, slot_params, ((1,), (1,)))
    return image_grad.astype(low), phi_grad, up_grad


def solution(mesh):
    fine = Mesh(mesh.devices.reshape([SIZES[name] for name in AXES]), AXES)
    group = ("y", "h")
    placed = (
        P(AXES, None),
        P(),
        P(OWNERS, None, group),
        P(OWNERS, group, None),
        P(AXES, None),
    )
    return jax.shard_map(
        local,
        mesh=fine,
        in_specs=placed,
        out_specs=(P(AXES, None), P(), P(OWNERS, group, None)),
        check_vma=False,
    )
```

```python
import jax
import jax.numpy as jnp
from jax import lax
from jax.sharding import Mesh, PartitionSpec as P

SLOT_EXP = 8
SIZES = {"y": 4, "h": 4, "x": 4, "l": 4, "c": 2}
AXES = ("y", "h", "x", "l", "c")
OWNERS = ("x", "l", "c")

cubic_coef = 0.044715
sqrt_ratio = 0.7978845608028654


def gelu_value(values):
    inner = sqrt_ratio * (values + cubic_coef * values * values * values)
    return 0.5 * values * (1.0 + jnp.tanh(inner))


def gelu_slope(values):
    tangent = jnp.tanh(sqrt_ratio * (values + cubic_coef * values * values * values))
    return 0.5 * (1.0 + tangent) + 0.5 * values * (1.0 - tangent * tangent) * sqrt_ratio * (
        1.0 + 3.0 * cubic_coef * values * values
    )


def mul(a, b, dims):
    return lax.dot_general(a, b, (dims, ((), ())), preferred_element_type=jnp.float32)


def shift(values, axis, step):
    size = lax.axis_size(axis)
    return lax.ppermute(values, axis, [(i, (i + step) % size) for i in range(size)])


def sum_hidden(terms):
    here = lax.axis_index("h")

    def chunk(offset):
        return lax.dynamic_index_in_dim(terms, (here + offset) % 4, 1, keepdims=False)

    def add(one, other):
        return (one.astype(jnp.float32) + other.astype(jnp.float32)).astype(terms.dtype)

    far, right, left = chunk(2), chunk(1), chunk(3)
    far_right = shift(far[:2], "h", 1)
    far_left = shift(far[2:], "h", -1)
    right = shift(jnp.concatenate([add(right[:2], far_right), right[2:]]), "h", 1)
    left = shift(jnp.concatenate([left[:2], add(left[2:], far_left)]), "h", -1)
    total = chunk(0).astype(jnp.float32) + right.astype(jnp.float32) + left.astype(jnp.float32)
    return total.astype(terms.dtype)


def pair(first, second, axis=0):
    shape = first.shape[:axis] + (2,) + first.shape[axis:]
    both = jnp.zeros(shape, first.dtype)
    both = lax.dynamic_update_slice_in_dim(both, jnp.expand_dims(first, axis), 0, axis)
    return lax.dynamic_update_slice_in_dim(both, jnp.expand_dims(second, axis), 1, axis)


def spread_rows(terms):
    here = lax.axis_index("y")
    blocks = []
    for step in range(4):
        block = lax.dynamic_index_in_dim(terms, (here + step) % 4, 0, keepdims=False)
        blocks.append(shift(block, "y", step) if step else block)
    return blocks


def everywhere(values, axes, count):
    spread = jnp.broadcast_to(values[None], (count,) + values.shape)
    return lax.all_to_all(spread, axes, 0, 0)


def local(patches, slot_params, up_weight, down_weight, output_grad):
    width = patches.shape[1]
    slots = slot_params.shape[1]
    owners = slots // SLOT_EXP
    shard = up_weight.shape[2]
    low = jnp.bfloat16

    logits = mul(patches, slot_params, ((1,), (0,)))
    dispatch = jax.nn.softmax(logits, axis=0)
    combine = jax.nn.softmax(logits, axis=1)
    dispatch_low = dispatch.astype(low)
    combine_low = combine.astype(low)
    slots_in = mul(dispatch_low, patches, ((0,), (0,))).astype(low)
    slot_grads = mul(combine_low, output_grad, ((0,), (0,))).astype(low)

    both = jnp.stack([slots_in, slot_grads]).reshape(2, owners, SLOT_EXP, width)
    landed = lax.all_to_all(both, OWNERS, 1, 1, tiled=True).reshape(2, slots, width)
    up_rows = lax.all_gather(up_weight[0].T, "h").reshape(4 * shard, width)
    landed, up_rows, down_rows = lax.optimization_barrier((landed, up_rows, down_weight[0]))
    down_rows = lax.all_gather(down_rows, "h").reshape(4 * shard, width)
    rows = everywhere(landed, "y", 4)
    rows_in = rows[:, 0].reshape(4 * slots, width)
    grads_in = rows[:, 1].reshape(4 * slots, width)

    hidden = mul(rows_in, up_rows, ((1,), (1,)))
    act_grad = mul(grads_in, down_rows, ((1,), (1,)))
    activation = gelu_value(hidden).astype(low)
    hidden_grad = (act_grad * gelu_slope(hidden)).astype(low)
    part_out = mul(activation, down_rows, ((1,), (0,))).astype(low)
    part_in = mul(hidden_grad, up_rows, ((1,), (0,))).astype(low)
    parts = jnp.stack([part_out.reshape(4, slots, width), part_in.reshape(4, slots, width)], axis=1)
    parts = lax.all_to_all(parts, "y", 0, 0).reshape(4, 2, owners, SLOT_EXP, width)
    summed = jnp.sum(parts.astype(jnp.float32), axis=0).astype(low)
    summed = jnp.swapaxes(summed, 0, 1)
    up_term = mul(rows_in, hidden_grad, ((0,), (0,))).astype(low)
    up_sum = sum_hidden(up_term.reshape(4, 4, width // 16, 4 * shard))
    summed, up_sum = lax.optimization_barrier((summed, up_sum))
    up_blocks = spread_rows(up_sum)
    back = lax.all_to_all(summed, OWNERS, 0, 0)
    back, up_blocks = lax.optimization_barrier((back, up_blocks))
    slot_out = back[:, 0].reshape(slots, width)
    slot_in_grad = back[:, 1].reshape(slots, width)


    dcombine = mul(output_grad, slot_out, ((1,), (1,)))
    ddispatch = mul(patches, slot_in_grad, ((1,), (1,)))
    logit_grad = dispatch * (ddispatch - jnp.sum(dispatch * ddispatch, axis=0, keepdims=True))
    logit_grad = logit_grad + combine * (
        dcombine - jnp.sum(combine * dcombine, axis=1, keepdims=True)
    )
    logit_low = logit_grad.astype(low)

    phi_term = mul(patches, logit_low, ((0,), (0,))).astype(low)
    pieces = SIZES["y"] * SIZES["x"] * SIZES["c"]
    piece = phi_term.reshape(pieces // 2, 2 * width // pieces, 2, slots // 2)
    piece = jnp.transpose(piece, (2, 0, 1, 3)).reshape(pieces, 2 * width // pieces, slots // 2)
    piece = jnp.sum(lax.all_to_all(piece, ("y", "x", "c"), 0, 0).astype(jnp.float32), axis=0)
    piece = everywhere(piece.astype(low), ("h", "l"), SIZES["h"] * SIZES["l"])
    piece = jnp.sum(piece.astype(jnp.float32), axis=0)
    here = lax.axis_index("y")
    up_grad = jnp.concatenate(
        [lax.select_n((here - source) % 4, *up_blocks) for source in range(4)], axis=1
    )[None]
    phi_grad = everywhere(piece.astype(low), ("y", "x", "c"), pieces)
    phi_grad = phi_grad.reshape(2, width, slots // 2).astype(jnp.float32)
    phi_grad = jnp.concatenate([phi_grad[0], phi_grad[1]], axis=1)

    image_grad = mul(dispatch_low, slot_in_grad, ((1,), (0,)))
    image_grad = image_grad + mul(logit_low, slot_params, ((1,), (1,)))
    return image_grad.astype(low), phi_grad, up_grad


def solution(mesh):
    fine = Mesh(mesh.devices.reshape([SIZES[name] for name in AXES]), AXES)
    group = ("y", "h")
    placed = (
        P(AXES, None),
        P(),
        P(OWNERS, None, group),
        P(OWNERS, group, None),
        P(AXES, None),
    )
    return jax.shard_map(
        local,
        mesh=fine,
        in_specs=placed,
        out_specs=(P(AXES, None), P(), P(OWNERS, group, None)),
        check_vma=False,
    )
```

```python
import jax
import jax.numpy as jnp
from jax import lax
from jax.sharding import Mesh, PartitionSpec as P

SLOT_EXP = 8
SIZES = {"y": 4, "h": 4, "x": 4, "l": 4, "c": 2}
AXES = ("y", "h", "x", "l", "c")
OWNERS = ("x", "l", "c")

cubic_coef = 0.044715
sqrt_ratio = 0.7978845608028654


def gelu_value(values):
    inner = sqrt_ratio * (values + cubic_coef * values * values * values)
    return 0.5 * values * (1.0 + jnp.tanh(inner))


def gelu_slope(values):
    tangent = jnp.tanh(sqrt_ratio * (values + cubic_coef * values * values * values))
    return 0.5 * (1.0 + tangent) + 0.5 * values * (1.0 - tangent * tangent) * sqrt_ratio * (
        1.0 + 3.0 * cubic_coef * values * values
    )


def mul(a, b, dims):
    return lax.dot_general(a, b, (dims, ((), ())), preferred_element_type=jnp.float32)


def shift(values, axis, step):
    size = lax.axis_size(axis)
    return lax.ppermute(values, axis, [(i, (i + step) % size) for i in range(size)])


def sum_hidden(terms):
    here = lax.axis_index("h")

    def chunk(offset):
        return lax.dynamic_index_in_dim(terms, (here + offset) % 4, 1, keepdims=False)

    def add(one, other):
        return (one.astype(jnp.float32) + other.astype(jnp.float32)).astype(terms.dtype)

    far, right, left = chunk(2), chunk(1), chunk(3)
    far_right = shift(far[:2], "h", 1)
    far_left = shift(far[2:], "h", -1)
    right = shift(jnp.concatenate([add(right[:2], far_right), right[2:]]), "h", 1)
    left = shift(jnp.concatenate([left[:2], add(left[2:], far_left)]), "h", -1)
    total = chunk(0).astype(jnp.float32) + right.astype(jnp.float32) + left.astype(jnp.float32)
    return total.astype(terms.dtype)


def spread_rows(terms):
    here = lax.axis_index("y")
    blocks = []
    for step in range(4):
        block = lax.dynamic_index_in_dim(terms, (here + step) % 4, 0, keepdims=False)
        blocks.append(shift(block, "y", step) if step else block)
    return blocks


def everywhere(values, axes, count):
    spread = jnp.broadcast_to(values[None], (count,) + values.shape)
    return lax.all_to_all(spread, axes, 0, 0)


def local(patches, slot_params, up_weight, down_weight, output_grad):
    width = patches.shape[1]
    slots = slot_params.shape[1]
    owners = slots // SLOT_EXP
    shard = up_weight.shape[2]
    low = jnp.bfloat16

    logits = mul(patches, slot_params, ((1,), (0,)))
    dispatch = jax.nn.softmax(logits, axis=0)
    combine = jax.nn.softmax(logits, axis=1)
    dispatch_low = dispatch.astype(low)
    combine_low = combine.astype(low)
    slots_in = mul(dispatch_low, patches, ((0,), (0,))).astype(low)
    slot_grads = mul(combine_low, output_grad, ((0,), (0,))).astype(low)

    both = jnp.stack([slots_in, slot_grads]).reshape(2, owners, SLOT_EXP, width)
    landed = lax.all_to_all(both, OWNERS, 1, 1, tiled=True).reshape(2, slots, width)
    up_rows = lax.all_gather(up_weight[0].T, "h").reshape(4 * shard, width)
    landed, up_rows, down_rows = lax.optimization_barrier((landed, up_rows, down_weight[0]))
    down_rows = lax.all_gather(down_rows, "h").reshape(4 * shard, width)
    rows = everywhere(landed, "y", 4)
    rows_in = rows[:, 0].reshape(4 * slots, width)
    grads_in = rows[:, 1].reshape(4 * slots, width)

    hidden = mul(rows_in, up_rows, ((1,), (1,)))
    act_grad = mul(grads_in, down_rows, ((1,), (1,)))
    activation = gelu_value(hidden).astype(low)
    hidden_grad = (act_grad * gelu_slope(hidden)).astype(low)
    part_out = mul(activation, down_rows, ((1,), (0,))).astype(low)
    part_in = mul(hidden_grad, up_rows, ((1,), (0,))).astype(low)
    blocks = (4, owners, SLOT_EXP, width)
    parts = jnp.stack([part_out.reshape(blocks), part_in.reshape(blocks)], axis=2)
    up_term = mul(rows_in, hidden_grad, ((0,), (0,))).astype(low)
    parts, up_term = lax.optimization_barrier((parts, up_term))
    parts = lax.all_to_all(parts, "y", 0, 0)
    summed = jnp.sum(parts.astype(jnp.float32), axis=0).astype(low)
    up_sum = sum_hidden(up_term.reshape(4, 4, width // 16, 4 * shard))
    summed, up_sum = lax.optimization_barrier((summed, up_sum))
    up_blocks = spread_rows(up_sum)
    back = lax.all_to_all(summed, OWNERS, 0, 0)
    back, up_blocks = lax.optimization_barrier((back, up_blocks))
    slot_out = back[:, 0].reshape(slots, width)
    slot_in_grad = back[:, 1].reshape(slots, width)


    dcombine = mul(output_grad, slot_out, ((1,), (1,)))
    ddispatch = mul(patches, slot_in_grad, ((1,), (1,)))
    logit_grad = dispatch * (ddispatch - jnp.sum(dispatch * ddispatch, axis=0, keepdims=True))
    logit_grad = logit_grad + combine * (
        dcombine - jnp.sum(combine * dcombine, axis=1, keepdims=True)
    )
    logit_low = logit_grad.astype(low)

    phi_term = mul(patches, logit_low, ((0,), (0,))).astype(low)
    pieces = SIZES["y"] * SIZES["x"] * SIZES["c"]
    piece = phi_term.reshape(pieces // 2, 2 * width // pieces, 2, slots // 2)
    piece = jnp.transpose(piece, (2, 0, 1, 3)).reshape(pieces, 2 * width // pieces, slots // 2)
    piece = jnp.sum(lax.all_to_all(piece, ("y", "x", "c"), 0, 0).astype(jnp.float32), axis=0)
    piece = everywhere(piece.astype(low), ("h", "l"), SIZES["h"] * SIZES["l"])
    piece = jnp.sum(piece.astype(jnp.float32), axis=0)
    here = lax.axis_index("y")
    up_grad = jnp.concatenate(
        [lax.select_n((here - source) % 4, *up_blocks) for source in range(4)], axis=1
    )[None]
    phi_grad = everywhere(piece.astype(low), ("y", "x", "c"), pieces)
    phi_grad = phi_grad.reshape(2, width, slots // 2).astype(jnp.float32)
    phi_grad = jnp.concatenate([phi_grad[0], phi_grad[1]], axis=1)

    image_grad = mul(dispatch_low, slot_in_grad, ((1,), (0,)))
    image_grad = image_grad + mul(logit_low, slot_params, ((1,), (1,)))
    return image_grad.astype(low), phi_grad, up_grad


def solution(mesh):
    fine = Mesh(mesh.devices.reshape([SIZES[name] for name in AXES]), AXES)
    group = ("y", "h")
    placed = (
        P(AXES, None),
        P(),
        P(OWNERS, None, group),
        P(OWNERS, group, None),
        P(AXES, None),
    )
    return jax.shard_map(
        local,
        mesh=fine,
        in_specs=placed,
        out_specs=(P(AXES, None), P(), P(OWNERS, group, None)),
        check_vma=False,
    )
```
